32 devices in a mesh: task: 4 (over y, x), shard: 8 (over z, core).
Axes of the slice: x: 2, y: 2, z: 4, core: 2. Of those that a mesh axis runs over, the one named last changes fastest.
Arguments:
- tokens: bfloat16 [1024, 4096], P(('task', 'shard')), may hold values from -600 to 600
- gain: float32 [4096], replicated, may hold values from 0.5 to 1.5
- task_ids: int32 [1024], P(('task', 'shard')), may hold values from 0 to 7, as said below
- order: int32 [1024], P(('task', 'shard')), may hold values from 0 to 31, as said below
- w_gate: bfloat16 [8, 4096, 14336], P('task', None, 'shard'), may hold values from -0.09375 to 0.09375
- w_up: bfloat16 [8, 4096, 14336], P('task', None, 'shard'), may hold values from -0.09375 to 0.09375
- w_down: bfloat16 [8, 14336, 4096], P('task', 'shard'), may hold values from -0.046875 to 0.046875
Outputs:
- mixed: bfloat16 [1024, 4096], P(('task', 'shard'))
The draws below stay inside these ranges and needn't reach their ends.
Inputs may be any that keep to these rules, and one draw needn't show every extreme that they name: `task_ids`: in each aligned block of 32 rows (the rows of one device) at most 8 rows name any one task; one task, the same for all blocks, is named by exactly 8 rows of every block. `order`: each aligned block of 32 entries is a permutation of 0 to 31.
All inputs are finite; a program needn't handle non-finite values.
Results may differ from the reference program's by a relative error of at most 0.015.
Values may be sent and summed in bfloat16 or wider, within the bound.
A program may use at most 192 MiB of HBM per device.

```python
import math
import jax
import jax.numpy as jnp
from jax import lax

D = 4096
FF = 14336
TOK_DEV = 32
CAP = 8
EXPERTS = 8
TOKENS = 1024
N_SHARD = 8


def draw_tokens(key, part):
    base_key, row_key, col_key = jax.random.split(jax.random.fold_in(key, 7), 3)
    base = jax.random.normal(base_key, (TOKENS, D), jnp.float32)
    base = jnp.clip(base, -6.0, 6.0)
    row_scale = jnp.exp(jax.random.uniform(row_key, (TOKENS, 1), jnp.float32) * math.log(10.0))
    col_scale = jnp.exp(jax.random.uniform(col_key, (1, D), jnp.float32) * math.log(10.0))
    return (base * row_scale * col_scale).astype(jnp.bfloat16)


def draw_task_ids(key, part):
    block_total = TOKENS // TOK_DEV
    heavy_key, block_key = jax.random.split(jax.random.fold_in(key, 101))
    heavy = jax.random.randint(heavy_key, (), 0, EXPERTS).astype(jnp.int32)
    labels = jnp.repeat(jnp.arange(EXPERTS - 1, dtype=jnp.int32), CAP)

    def one_block(single_key):
        choose_key, shuffle_key = jax.random.split(single_key)
        chosen = jax.random.permutation(choose_key, labels)[:TOK_DEV - CAP]
        others = jnp.where(chosen >= heavy, chosen + 1, chosen).astype(jnp.int32)
        filled = jnp.concatenate([jnp.full((CAP,), heavy, jnp.int32), others])
        return jax.random.permutation(shuffle_key, filled)
    blocks = jax.vmap(one_block)(jax.random.split(block_key, block_total))
    return blocks.reshape(TOKENS).astype(jnp.int32)


def draw_order(key, part):
    block_total = TOKENS // TOK_DEV
    base_key = jax.random.fold_in(key, 202)
    natural = jnp.arange(TOK_DEV, dtype=jnp.int32)

    def one_block(single_key):
        return jax.random.permutation(single_key, natural)
    blocks = jax.vmap(one_block)(jax.random.split(base_key, block_total))
    return blocks.reshape(TOKENS).astype(jnp.int32)


def level_of(stream_key, dims, pieces, smallest, top_value):
    def one(axis_at, shards_of):
        heights = jax.random.uniform(jax.random.fold_in(jax.random.fold_in(stream_key, 6), axis_at), (shards_of,), jnp.float32, smallest / len(pieces), top_value / len(pieces))
        return jnp.repeat(jnp.exp(heights), dims[axis_at] // shards_of).reshape((-1,) + (1,) * (len(dims) - axis_at - 1))

    level = one(*pieces[0])
    for cut in pieces[1:]:
        level = level * one(*cut)
    return level


def gaussian(own_key, dims, scale, bound, cuts=(), kind=jnp.bfloat16):
    drawn = jax.random.normal(own_key, dims, jnp.float32) * scale
    if len(cuts) > 0:
        drawn = level_of(own_key, dims, cuts, -0.22, 0.18) * drawn
    return jnp.clip(drawn, min=-bound, max=bound).astype(kind)


def setup_inputs(seed: int = 0) -> dict:
    arg_keys = jax.random.split(jax.random.key(seed), 8)
    return {
        "tokens": draw_tokens(jax.random.fold_in(arg_keys[7], 71), 0),
        "gain": jnp.clip(1.0 + 0.1 * jax.random.normal(arg_keys[1], (D,), jnp.float32), 0.5, 1.5),
        "task_ids": draw_task_ids(jax.random.fold_in(arg_keys[7], 71), 0),
        "order": draw_order(jax.random.fold_in(arg_keys[7], 71), 0),
        "w_gate": gaussian(arg_keys[4], (EXPERTS, D, FF), D ** -0.5, 0.09375, ((0, 4), (2, 8))),
        "w_up": gaussian(arg_keys[5], (EXPERTS, D, FF), D ** -0.5, 0.09375, ((0, 4), (2, 8))),
        "w_down": gaussian(arg_keys[6], (EXPERTS, FF, D), FF ** -0.5, 0.046875, ((0, 4), (1, 8))),
    }


def expert_rows(operand):
    rows_in, gate_weights, up_weights, down_weights = operand
    gate_value = jnp.dot(rows_in, gate_weights, preferred_element_type=jnp.float32)
    up_value = jnp.dot(rows_in, up_weights, preferred_element_type=jnp.float32)
    hidden = (jax.nn.silu(gate_value) * up_value).astype(jnp.bfloat16)
    row_total = hidden.shape[0]
    hidden_blocks = jnp.swapaxes(hidden.reshape(row_total, N_SHARD, FF // N_SHARD), 0, 1)
    down_blocks = down_weights.reshape(N_SHARD, FF // N_SHARD, D)

    def add_term(running, pair):
        term = jnp.dot(pair[0], pair[1], preferred_element_type=jnp.float32).astype(jnp.bfloat16)
        term = lax.optimization_barrier(term).astype(jnp.float32)
        return (running + term, None)
    start_sum = jnp.zeros((row_total, D), jnp.float32)
    summed, unused = lax.scan(add_term, start_sum, (hidden_blocks, down_blocks))
    return summed.astype(jnp.bfloat16)

def reference(tokens, gain, task_ids, order, w_gate, w_up, w_down):
    values = tokens.astype(jnp.float32)
    mean_square = lax.optimization_barrier(jnp.mean(values * values, axis=-1, keepdims=True))
    normed = (values * lax.rsqrt(mean_square + 1e-06) * gain).astype(jnp.bfloat16)
    block_total = TOKENS // TOK_DEV
    onehot = (task_ids[:, None] == jnp.arange(EXPERTS, dtype=jnp.int32)[None, :]).astype(jnp.int32)
    counted = jnp.cumsum(onehot.reshape(block_total, TOK_DEV, EXPERTS), axis=1).reshape(TOKENS, EXPERTS)
    position = (lax.optimization_barrier(jnp.sum(counted * onehot, axis=1)) - 1).astype(jnp.int32)
    block_index = (jnp.arange(TOKENS, dtype=jnp.int32) // TOK_DEV).astype(jnp.int32)
    per_expert = block_total * CAP
    slot_index = (task_ids * per_expert + block_index * CAP + position).astype(jnp.int32)
    buffered = jnp.zeros((EXPERTS * per_expert, D), jnp.bfloat16).at[slot_index].set(normed)
    buffered = buffered.reshape(EXPERTS, per_expert, D)
    served = lax.map(expert_rows, (buffered, w_gate, w_up, w_down))
    expert_out = served.reshape(EXPERTS * per_expert, D)[slot_index]
    source_rows = (block_index * TOK_DEV + order).astype(jnp.int32)
    return expert_out[source_rows]
```

```python
import functools

import jax
import jax.numpy as jnp
from jax import lax
from jax.experimental import pallas as pl
from jax.experimental.pallas import tpu as pltpu
from jax.sharding import PartitionSpec as P

MESH = pl.DeviceIdType.MESH
CAP = 8
CORES = 2
CHUNK = 1024
UP_SLOTS = 6
DOWN_SLOTS = 3
VMEM_BYTES = 63 * 2**20
epsilon = 1e-06


def tile_of(size):
    return 256 if size % 256 == 0 else size


def layer_kernel(
    tasks, chips, chunk,
    tokens, gain, task_col, task_row, order_col, w_gate, w_up, w_down, out,
    ids, rows, placed, x, gate_acc, up_acc, hidden, part, sib, pair, back, picked, terms, wbuf, dbuf,
    w_sem, d_sem, i_send, i_recv, z_send, z_recv, x_send, x_recv, x_local, b_send, b_recv,
    c_send, c_recv, y_send, y_recv, y_local, t_send, t_recv,
):
    experts, width, ff = w_gate.shape
    count = tokens.shape[0]
    chunks = width // chunk
    per = chips * CAP
    slots = tasks * experts * per
    tile = tile_of(ff)
    me_t = lax.axis_index("task")
    me_s = lax.axis_index("shard")
    me_q = me_s // CORES
    me_c = me_s % CORES
    other_c = 1 - me_c
    sibling = (me_t, me_q * CORES + other_c)

    def chip_at(k):
        return lax.rem(me_q + k, chips)

    def task_at(k):
        return lax.rem(me_t + k, tasks)

    up_pieces = [(j, e, w) for j in range(chunks) for e in range(experts) for w in (w_gate, w_up)]
    down_pieces = [(j, e) for j in range(chunks) for e in range(experts)]

    def up_copy(i):
        j, e, w = up_pieces[i]
        slot = i % UP_SLOTS
        return pltpu.make_async_copy(
            w.at[e, pl.ds(j * chunk, chunk), :], wbuf.at[slot], w_sem.at[slot]
        )

    def down_copy(i):
        j, e = down_pieces[i]
        slot = i % DOWN_SLOTS
        return pltpu.make_async_copy(
            w_down.at[e, :, pl.ds(j * chunk, chunk)], dbuf.at[slot], d_sem.at[slot]
        )

    barrier = pltpu.get_barrier_semaphore()
    chip_peers = [(me_t, chip_at(k) * CORES + me_c) for k in range(1, chips)]
    task_peers = [(task_at(k), me_s) for k in range(1, tasks)]
    for peer in chip_peers + task_peers + [sibling]:
        pl.semaphore_signal(barrier, inc=1, device_id=peer, device_id_type=MESH)

    for i in range(min(UP_SLOTS, len(up_pieces))):
        up_copy(i).start()
    for i in range(min(DOWN_SLOTS, len(down_pieces))):
        down_copy(i).start()

    col = jnp.broadcast_to(task_col[...], (count, count))
    row = jnp.broadcast_to(task_row[...], (count, count))
    first = lax.broadcasted_iota(jnp.int32, (count, count), 0)
    second = lax.broadcasted_iota(jnp.int32, (count, count), 1)
    same = col == row
    col_pos = jnp.sum(jnp.where(same & (second < first), 1.0, 0.0), axis=1, keepdims=True)
    row_pos = jnp.sum(jnp.where(same & (first < second), 1.0, 0.0), axis=0, keepdims=True)
    col_id = task_col[...].astype(jnp.float32) * CAP + col_pos
    row_id = task_row[...].astype(jnp.float32) * CAP + row_pos
    taken = jnp.broadcast_to(order_col[...], (count, count)) == second
    want_id = jnp.sum(
        jnp.where(taken, jnp.broadcast_to(row_id, (count, count)), 0.0), axis=1, keepdims=True
    )
    ids[me_q, 0] = jnp.broadcast_to(col_id, (count, 128))
    ids[me_q, 1] = jnp.broadcast_to(want_id, (count, 128))

    values = tokens[...].astype(jnp.float32)
    mean_square = jnp.mean(values * values, axis=-1, keepdims=True)
    scale = lax.rsqrt(mean_square + epsilon)
    for j in range(chunks):
        part_cols = pl.ds(j * chunk, chunk)
        rows[j, me_q] = (
            tokens[:, part_cols].astype(jnp.float32) * scale * gain[:, part_cols]
        ).astype(jnp.bfloat16)

    pl.semaphore_wait(barrier, len(chip_peers) + len(task_peers) + 1)

    sends = []

    def remote(src, dst, send, recv, peer):
        copy = pltpu.make_async_remote_copy(
            src_ref=src, dst_ref=dst, send_sem=send, recv_sem=recv,
            device_id=peer, device_id_type=MESH,
        )
        copy.start()
        sends.append(copy)
        return copy

    id_copies = [
        remote(ids.at[me_q], ids.at[me_q], i_send.at[k], i_recv.at[k], peer)
        for k, peer in enumerate(chip_peers)
    ]
    row_copies = [
        [
            remote(rows.at[j, me_q], rows.at[j, me_q], z_send.at[j, k], z_recv.at[j, k], peer)
            for k, peer in enumerate(chip_peers)
        ]
        for j in range(chunks)
    ]

    for copy in id_copies:
        copy.wait_recv()
    shape = (chips * count, slots)
    lane = lax.broadcasted_iota(jnp.int32, shape, 1)
    line = lax.broadcasted_iota(jnp.int32, shape, 0)
    lane_id = ((lane // per) * CAP + lane % CAP).astype(jnp.float32)
    mine = (lane // CAP) % chips == line // count

    def one_hot(which):
        held = ids[:, which].reshape(chips * count, 128)[:, :1]
        hit = (jnp.broadcast_to(held, shape) == lane_id) & mine
        return jnp.where(hit, 1.0, 0.0)

    placing = one_hot(0).T.astype(jnp.bfloat16)
    picking = one_hot(1).astype(jnp.bfloat16)

    cross, swaps, pair_swaps, returns, finals = {}, {}, {}, {}, {}

    def place(j):
        for copy in row_copies[j]:
            copy.wait_recv()
        for n in range(0, chunk, 256):
            got = jnp.dot(
                placing,
                rows[j, :, :, n : n + 256].reshape(chips * count, 256),
                preferred_element_type=jnp.float32,
            ).astype(jnp.bfloat16)
            placed[j, :, :, :, n : n + 256] = got.reshape(tasks, experts, per, 256)
        cross[j] = [
            remote(
                placed.at[j, peer[0]], x.at[j, :, me_c, me_t],
                x_send.at[j, k], x_recv.at[j, k], peer,
            )
            for k, peer in enumerate(task_peers)
        ]
        local = pltpu.make_async_copy(
            placed.at[j, me_t], x.at[j, :, me_c, me_t], x_local.at[j]
        )
        local.start()
        cross[j].append(local)

    def swap(j):
        for copy in cross[j][:-1]:
            copy.wait_recv()
        cross[j][-1].wait()
        swaps[j] = remote(
            x.at[j, :, me_c], x.at[j, :, me_c], b_send.at[j], b_recv.at[j], sibling
        )

    def enter(j):
        swaps[j].wait_recv()
        for e in range(experts):
            i = (j * experts + e) * 2
            up_copy(i).wait()
            up_copy(i + 1).wait()

            def step(n, carry):
                columns = pl.ds(pl.multiple_of(n * tile, tile), tile)
                block = x[j, e].reshape(CORES * tasks * per, chunk)
                g = jnp.dot(
                    block, wbuf[i % UP_SLOTS, :, columns], preferred_element_type=jnp.float32
                )
                u = jnp.dot(
                    block, wbuf[(i + 1) % UP_SLOTS, :, columns], preferred_element_type=jnp.float32
                )
                if j > 0:
                    g += gate_acc[e, :, columns]
                    u += up_acc[e, :, columns]
                if j < chunks - 1:
                    gate_acc[e, :, columns] = g
                    up_acc[e, :, columns] = u
                else:
                    hidden[e, :, columns] = (g / (1.0 + jnp.exp(-g)) * u).astype(jnp.bfloat16)
                return carry

            lax.fori_loop(0, ff // tile, step, 0)
            for later in (i + UP_SLOTS, i + 1 + UP_SLOTS):
                if later < len(up_pieces):
                    up_copy(later).start()

    def leave(j):
        for e in range(experts):
            i = j * experts + e
            down_copy(i).wait()

            def step(n, carry):
                columns = pl.ds(pl.multiple_of(n * 256, 256), 256)
                got = jnp.dot(
                    hidden[e], dbuf[i % DOWN_SLOTS, :, columns], preferred_element_type=jnp.float32
                ).astype(jnp.bfloat16)
                part[j, e, :, :, :, columns] = got.reshape(CORES, tasks, per, 256)
                return carry

            lax.fori_loop(0, chunk // 256, step, 0)
            if i + DOWN_SLOTS < len(down_pieces):
                down_copy(i + DOWN_SLOTS).start()
        pair_swaps[j] = remote(
            part.at[j, :, other_c], sib.at[j], c_send.at[j], c_recv.at[j], sibling
        )

    def add_pair(j):
        pair_swaps[j].wait_recv()
        for e in range(experts):
            for t in range(tasks):
                pair[j, e, t] = (
                    part[j, e, me_c, t].astype(jnp.float32) + sib[j, e, t].astype(jnp.float32)
                ).astype(jnp.bfloat16)
        returns[j] = [
            remote(
                pair.at[j, :, peer[0]], back.at[j, me_t], y_send.at[j, k], y_recv.at[j, k], peer
            )
            for k, peer in enumerate(task_peers)
        ]
        local = pltpu.make_async_copy(pair.at[j, :, me_t], back.at[j, me_t], y_local.at[j])
        local.start()
        returns[j].append(local)

    def pick(j):
        for copy in returns[j][:-1]:
            copy.wait_recv()
        returns[j][-1].wait()
        for n in range(0, chunk, 256):
            got = jnp.dot(
                picking,
                back[j, :, :, :, n : n + 256].reshape(slots, 256),
                preferred_element_type=jnp.float32,
            ).astype(jnp.bfloat16)
            picked[j, :, :, n : n + 256] = got.reshape(chips, count, 256)
        finals[j] = [
            remote(
                picked.at[j, chip_at(k + 1)], terms.at[j, me_q],
                t_send.at[j, k], t_recv.at[j, k], peer,
            )
            for k, peer in enumerate(chip_peers)
        ]
        terms[j, me_q] = picked[j, me_q]

    def finish(j):
        for copy in finals[j]:
            copy.wait_recv()
        total = terms[j, 0].astype(jnp.float32)
        for k in range(1, chips):
            total += terms[j, k].astype(jnp.float32)
        out[:, pl.ds(j * chunk, chunk)] = total.astype(jnp.bfloat16)

    for step in range(chunks + 2):
        if step < chunks:
            place(step)
        if 0 <= step - 1 < chunks:
            swap(step - 1)
        if 0 <= step - 2 < chunks:
            enter(step - 2)
    for step in range(chunks + 3):
        if step < chunks:
            leave(step)
        if 0 <= step - 1 < chunks:
            add_pair(step - 1)
        if 0 <= step - 2 < chunks:
            pick(step - 2)
        if 0 <= step - 3 < chunks:
            finish(step - 3)
    for copy in sends:
        copy.wait_send()


def scratch_of(tasks, chips, chunk, tokens, w_gate):
    experts, width, ff = w_gate.shape
    count = tokens.shape[0]
    chunks, per = width // chunk, chips * CAP
    bf16, f32 = jnp.bfloat16, jnp.float32
    group = CORES * tasks * per
    buffers = [
        ((chips, 2, count, 128), f32),
        ((chunks, chips, count, chunk), bf16),
        ((chunks, tasks, experts, per, chunk), bf16),
        ((chunks, experts, CORES, tasks, per, chunk), bf16),
        ((experts, group, ff), f32),
        ((experts, group, ff), f32),
        ((experts, group, ff), bf16),
        ((chunks, experts, CORES, tasks, per, chunk), bf16),
        ((chunks, experts, tasks, per, chunk), bf16),
        ((chunks, experts, tasks, per, chunk), bf16),
        ((chunks, tasks, experts, per, chunk), bf16),
        ((chunks, chips, count, chunk), bf16),
        ((chunks, chips, count, chunk), bf16),
        ((UP_SLOTS, chunk, ff), bf16),
        ((DOWN_SLOTS, ff, chunk), bf16),
    ]
    size = sum(functools.reduce(lambda a, b: a * b, s) * jnp.dtype(d).itemsize for s, d in buffers)
    dma = pltpu.SemaphoreType.DMA
    sems = [dma((UP_SLOTS,)), dma((DOWN_SLOTS,)), dma((chips,)), dma((chips,))]
    sems += [dma((chunks, chips))] * 2 + [dma((chunks, tasks))] * 2 + [dma((chunks,))] * 5
    sems += [dma((chunks, tasks))] * 2 + [dma((chunks,))] + [dma((chunks, chips))] * 2
    return [pltpu.VMEM(s, d) for s, d in buffers] + sems, size


def fused(tokens, gain, task_ids, order, w_gate, w_up, w_down, scratch, chunk):
    tasks, chips = lax.axis_size("task"), lax.axis_size("shard") // CORES
    count, width = tokens.shape
    vmem = pl.BlockSpec(memory_space=pltpu.VMEM)
    hbm = pl.BlockSpec(memory_space=pl.ANY)
    return pl.pallas_call(
        functools.partial(layer_kernel, tasks, chips, chunk),
        out_shape=jax.ShapeDtypeStruct((count, width), jnp.bfloat16),
        in_specs=[vmem] * 5 + [hbm] * 3,
        out_specs=vmem,
        scratch_shapes=scratch,
        compiler_params=pltpu.CompilerParams(
            collective_id=0, has_side_effects=True, vmem_limit_bytes=VMEM_BYTES
        ),
        name="expert_layer",
    )(
        tokens, gain.reshape(1, width), task_ids.reshape(count, 1), task_ids.reshape(1, count),
        order.reshape(count, 1), w_gate, w_up, w_down,
    )


def expert_block(gathered_rows, w_gate, w_up, w_down):
    gate_value = jnp.einsum(
        "red,edf->ref", gathered_rows, w_gate, preferred_element_type=jnp.float32
    )
    up_value = jnp.einsum("red,edf->ref", gathered_rows, w_up, preferred_element_type=jnp.float32)
    hidden = (jax.nn.silu(gate_value) * up_value).astype(jnp.bfloat16)
    return jnp.einsum("ref,efd->red", hidden, w_down, preferred_element_type=jnp.float32)


def collective(tokens, gain, task_ids, order, w_gate, w_up, w_down):
    task_count = lax.axis_size("task")
    local_experts = w_gate.shape[0]
    expert_count = task_count * local_experts
    feature_count = tokens.shape[1]
    values = tokens.astype(jnp.float32)
    mean_square = jnp.mean(values * values, axis=-1, keepdims=True)
    normed = (values * lax.rsqrt(mean_square + epsilon) * gain).astype(jnp.bfloat16)
    onehot = (task_ids[:, None] == jnp.arange(expert_count, dtype=jnp.int32)[None, :]).astype(
        jnp.int32
    )
    position = jnp.sum(jnp.cumsum(onehot, axis=0) * onehot, axis=1) - 1
    slot_index = (
        task_ids // local_experts * CAP + position
    ) * local_experts + task_ids % local_experts
    slot_count = task_count * CAP * local_experts
    slot_range = jnp.arange(slot_count, dtype=jnp.int32)
    placing = (slot_index[:, None] == slot_range[None, :]).astype(jnp.bfloat16)
    outgoing = jnp.einsum("rs,rd->sd", placing, normed, preferred_element_type=jnp.float32).astype(
        jnp.bfloat16
    )
    outgoing = outgoing.reshape(task_count, CAP, local_experts, feature_count)
    arrived = lax.all_to_all(outgoing, "task", split_axis=0, concat_axis=0, tiled=True)
    local_rows = arrived.reshape(task_count * CAP, local_experts, feature_count)
    partial_terms = expert_block(
        lax.all_gather(local_rows, "shard", axis=0, tiled=True), w_gate, w_up, w_down
    )
    summed = lax.psum_scatter(
        partial_terms.astype(jnp.bfloat16), "shard", scatter_dimension=0, tiled=True
    )
    results = summed.reshape(task_count, CAP, local_experts, feature_count)
    returned = lax.all_to_all(results, "task", split_axis=0, concat_axis=0, tiled=True)
    returned = returned.reshape(slot_count, feature_count)
    wanted = jnp.take(slot_index, order)
    selecting = (wanted[:, None] == slot_range[None, :]).astype(jnp.bfloat16)
    return jnp.dot(selecting, returned, preferred_element_type=jnp.float32).astype(jnp.bfloat16)


def shards(tokens, gain, task_ids, order, w_gate, w_up, w_down):
    tasks, shard_count = lax.axis_size("task"), lax.axis_size("shard")
    width = tokens.shape[1]
    chunk = CHUNK if width % CHUNK == 0 else width
    chips = shard_count // CORES
    scratch, size = scratch_of(tasks, chips, chunk, tokens, w_gate)
    arrays = (tokens, gain, task_ids, order, w_gate, w_up, w_down)
    if shard_count % CORES or chunk % 256 or size + 2 * 2**20 > VMEM_BYTES:
        return collective(*arrays)
    return fused(*arrays, scratch, chunk)


def solution(mesh):
    placed = (
        P(("task", "shard"), None),
        P(),
        P(("task", "shard")),
        P(("task", "shard")),
        P("task", None, "shard"),
        P("task", None, "shard"),
        P("task", "shard", None),
    )
    return jax.shard_map(
        shards, mesh=mesh, in_specs=placed, out_specs=P(("task", "shard"), None), check_vma=False
    )
```

```python
import functools

import jax
import jax.numpy as jnp
from jax import lax
from jax.experimental import pallas as pl
from jax.experimental.pallas import tpu as pltpu
from jax.sharding import PartitionSpec as P

MESH = pl.DeviceIdType.MESH
CAP = 8
CORES = 2
CHUNK = 1024
UP_SLOTS = 6
DOWN_SLOTS = 3
AHEAD = 2
VMEM_BYTES = 63 * 2**20
epsilon = 1e-06


def tile_of(size):
    return 256 if size % 256 == 0 else size


def layer_kernel(
    tasks, chips, chunk,
    tokens, gain, task_row, order_row, w_gate, w_up, w_down, out,
    ids, rows, placed, x, gate_acc, up_acc, hidden, part, sib, pair, back, picked, terms, wbuf, dbuf,
    w_sem, d_sem, i_send, i_recv, z_send, z_recv, x_send, x_recv, x_local, b_send, b_recv,
    c_send, c_recv, y_send, y_recv, y_local, t_send, t_recv,
):
    experts, width, ff = w_gate.shape
    count = tokens.shape[0]
    chunks = width // chunk
    per = chips * CAP
    slots = tasks * experts * per
    tile = tile_of(ff)
    me_t = lax.axis_index("task")
    me_s = lax.axis_index("shard")
    me_q = me_s // CORES
    me_c = me_s % CORES
    other_c = 1 - me_c
    sibling = (me_t, me_q * CORES + other_c)

    def chip_at(k):
        return lax.rem(me_q + k, chips)

    def task_at(k):
        return lax.rem(me_t + k, tasks)

    up_pieces = [(j, e, w) for j in range(chunks) for e in range(experts) for w in (w_gate, w_up)]
    down_pieces = [(j, e) for j in range(chunks) for e in range(experts)]

    def up_copy(i):
        j, e, w = up_pieces[i]
        slot = i % UP_SLOTS
        return pltpu.make_async_copy(
            w.at[e, pl.ds(j * chunk, chunk), :], wbuf.at[slot], w_sem.at[slot]
        )

    def down_copy(i):
        j, e = down_pieces[i]
        slot = i % DOWN_SLOTS
        return pltpu.make_async_copy(
            w_down.at[e, :, pl.ds(j * chunk, chunk)], dbuf.at[slot], d_sem.at[slot]
        )

    barrier = pltpu.get_barrier_semaphore()
    chip_peers = [(me_t, chip_at(k) * CORES + me_c) for k in range(1, chips)]
    task_peers = [(task_at(k), me_s) for k in range(1, tasks)]
    for peer in chip_peers + task_peers + [sibling]:
        pl.semaphore_signal(barrier, inc=1, device_id=peer, device_id_type=MESH)

    for i in range(min(UP_SLOTS, len(up_pieces))):
        up_copy(i).start()
    for i in range(min(DOWN_SLOTS, len(down_pieces))):
        down_copy(i).start()

    first = lax.broadcasted_iota(jnp.int32, (count, count), 0)
    second = lax.broadcasted_iota(jnp.int32, (count, count), 1)
    task_line = task_row[...].astype(jnp.float32)
    order_line = order_row[...].astype(jnp.float32)

    def as_column(line):
        spread = jnp.broadcast_to(line, (count, count))
        return jnp.sum(jnp.where(first == second, spread, 0.0), axis=1, keepdims=True)

    task_col = as_column(task_line)
    order_col = as_column(order_line)
    col = jnp.broadcast_to(task_col, (count, count))
    row = jnp.broadcast_to(task_line, (count, count))
    same = col == row
    col_pos = jnp.sum(jnp.where(same & (second < first), 1.0, 0.0), axis=1, keepdims=True)
    row_pos = jnp.sum(jnp.where(same & (first < second), 1.0, 0.0), axis=0, keepdims=True)
    col_id = task_col * CAP + col_pos
    row_id = task_line * CAP + row_pos
    taken = jnp.broadcast_to(order_col, (count, count)) == second.astype(jnp.float32)
    want_id = jnp.sum(
        jnp.where(taken, jnp.broadcast_to(row_id, (count, count)), 0.0), axis=1, keepdims=True
    )
    ids[me_q, 0] = jnp.broadcast_to(col_id, (count, 128))
    ids[me_q, 1] = jnp.broadcast_to(want_id, (count, 128))

    values = tokens[...].astype(jnp.float32)
    mean_square = jnp.mean(values * values, axis=-1, keepdims=True)
    scale = lax.rsqrt(mean_square + epsilon)
    for j in range(chunks):
        part_cols = pl.ds(j * chunk, chunk)
        rows[j, me_q] = (
            tokens[:, part_cols].astype(jnp.float32) * scale * gain[:, part_cols]
        ).astype(jnp.bfloat16)

    pl.semaphore_wait(barrier, len(chip_peers) + len(task_peers) + 1)

    sends = []

    def remote(src, dst, send, recv, peer):
        copy = pltpu.make_async_remote_copy(
            src_ref=src, dst_ref=dst, send_sem=send, recv_sem=recv,
            device_id=peer, device_id_type=MESH,
        )
        copy.start()
        sends.append(copy)
        return copy

    id_copies = [
        remote(ids.at[me_q], ids.at[me_q], i_send.at[k], i_recv.at[k], peer)
        for k, peer in enumerate(chip_peers)
    ]
    row_copies = {}

    def send_rows(j):
        row_copies[j] = [
            remote(rows.at[j, me_q], rows.at[j, me_q], z_send.at[j, k], z_recv.at[j, k], peer)
            for k, peer in enumerate(chip_peers)
        ]

    for j in range(min(AHEAD, chunks)):
        send_rows(j)

    for copy in id_copies:
        copy.wait_recv()
    shape = (chips * count, slots)
    lane = lax.broadcasted_iota(jnp.int32, shape, 1)
    line = lax.broadcasted_iota(jnp.int32, shape, 0)
    lane_id = ((lane // per) * CAP + lane % CAP).astype(jnp.float32)
    mine = (lane // CAP) % chips == line // count

    def one_hot(which):
        held = ids[:, which].reshape(chips * count, 128)[:, :1]
        hit = (jnp.broadcast_to(held, shape) == lane_id) & mine
        return jnp.where(hit, 1.0, 0.0)

    placing = one_hot(0).T.astype(jnp.bfloat16)
    picking = one_hot(1).astype(jnp.bfloat16)

    cross, swaps, pair_swaps, returns, finals = {}, {}, {}, {}, {}

    def place(j):
        for copy in row_copies[j]:
            copy.wait_recv()
        if j + AHEAD < chunks:
            send_rows(j + AHEAD)
        for n in range(0, chunk, 256):
            got = jnp.dot(
                placing,
                rows[j, :, :, n : n + 256].reshape(chips * count, 256),
                preferred_element_type=jnp.float32,
            ).astype(jnp.bfloat16)
            placed[j, :, :, :, n : n + 256] = got.reshape(tasks, experts, per, 256)
        cross[j] = [
            remote(
                placed.at[j, peer[0]], x.at[j, :, me_c, me_t],
                x_send.at[j, k], x_recv.at[j, k], peer,
            )
            for k, peer in enumerate(task_peers)
        ]
        local = pltpu.make_async_copy(
            placed.at[j, me_t], x.at[j, :, me_c, me_t], x_local.at[j]
        )
        local.start()
        cross[j].append(local)

    def swap(j):
        for copy in cross[j][:-1]:
            copy.wait_recv()
        cross[j][-1].wait()
        swaps[j] = remote(
            x.at[j, :, me_c], x.at[j, :, me_c], b_send.at[j], b_recv.at[j], sibling
        )

    def enter(j):
        swaps[j].wait_recv()
        for e in range(experts):
            i = (j * experts + e) * 2
            up_copy(i).wait()
            up_copy(i + 1).wait()

            def step(n, carry):
                columns = pl.ds(pl.multiple_of(n * tile, tile), tile)
                block = x[j, e].reshape(CORES * tasks * per, chunk)
                g = jnp.dot(
                    block, wbuf[i % UP_SLOTS, :, columns], preferred_element_type=jnp.float32
                )
                u = jnp.dot(
                    block, wbuf[(i + 1) % UP_SLOTS, :, columns], preferred_element_type=jnp.float32
                )
                if j > 0:
                    g += gate_acc[e, :, columns]
                    u += up_acc[e, :, columns]
                if j < chunks - 1:
                    gate_acc[e, :, columns] = g
                    up_acc[e, :, columns] = u
                else:
                    hidden[e, :, columns] = (g / (1.0 + jnp.exp(-g)) * u).astype(jnp.bfloat16)
                return carry

            lax.fori_loop(0, ff // tile, step, 0)
            for later in (i + UP_SLOTS, i + 1 + UP_SLOTS):
                if later < len(up_pieces):
                    up_copy(later).start()

    def leave(j):
        for e in range(experts):
            i = j * experts + e
            down_copy(i).wait()

            def step(n, carry):
                columns = pl.ds(pl.multiple_of(n * 256, 256), 256)
                got = jnp.dot(
                    hidden[e], dbuf[i % DOWN_SLOTS, :, columns], preferred_element_type=jnp.float32
                ).astype(jnp.bfloat16)
                part[j, e, :, :, :, columns] = got.reshape(CORES, tasks, per, 256)
                return carry

            lax.fori_loop(0, chunk // 256, step, 0)
            if i + DOWN_SLOTS < len(down_pieces):
                down_copy(i + DOWN_SLOTS).start()
        pair_swaps[j] = remote(
            part.at[j, :, other_c], sib.at[j], c_send.at[j], c_recv.at[j], sibling
        )

    def add_pair(j):
        pair_swaps[j].wait_recv()
        for e in range(experts):
            for t in range(tasks):
                pair[j, e, t] = (
                    part[j, e, me_c, t].astype(jnp.float32) + sib[j, e, t].astype(jnp.float32)
                ).astype(jnp.bfloat16)
        returns[j] = [
            remote(
                pair.at[j, :, peer[0]], back.at[j, me_t], y_send.at[j, k], y_recv.at[j, k], peer
            )
            for k, peer in enumerate(task_peers)
        ]
        local = pltpu.make_async_copy(pair.at[j, :, me_t], back.at[j, me_t], y_local.at[j])
        local.start()
        returns[j].append(local)

    def pick(j):
        for copy in returns[j][:-1]:
            copy.wait_recv()
        returns[j][-1].wait()
        for n in range(0, chunk, 256):
            got = jnp.dot(
                picking,
                back[j, :, :, :, n : n + 256].reshape(slots, 256),
                preferred_element_type=jnp.float32,
            ).astype(jnp.bfloat16)
            picked[j, :, :, n : n + 256] = got.reshape(chips, count, 256)
        finals[j] = [
            remote(
                picked.at[j, chip_at(k + 1)], terms.at[j, me_q],
                t_send.at[j, k], t_recv.at[j, k], peer,
            )
            for k, peer in enumerate(chip_peers)
        ]
        terms[j, me_q] = picked[j, me_q]

    def finish(j):
        for copy in finals[j]:
            copy.wait_recv()
        total = terms[j, 0].astype(jnp.float32)
        for k in range(1, chips):
            total += terms[j, k].astype(jnp.float32)
        out[:, pl.ds(j * chunk, chunk)] = total.astype(jnp.bfloat16)

    for step in range(chunks + 2):
        if step < chunks:
            place(step)
        if 0 <= step - 1 < chunks:
            swap(step - 1)
        if 0 <= step - 2 < chunks:
            enter(step - 2)
    for step in range(chunks + 3):
        if step < chunks:
            leave(step)
        if 0 <= step - 1 < chunks:
            add_pair(step - 1)
        if 0 <= step - 2 < chunks:
            pick(step - 2)
        if 0 <= step - 3 < chunks:
            finish(step - 3)
    for copy in sends:
        copy.wait_send()


def scratch_of(tasks, chips, chunk, tokens, w_gate):
    experts, width, ff = w_gate.shape
    count = tokens.shape[0]
    chunks, per = width // chunk, chips * CAP
    bf16, f32 = jnp.bfloat16, jnp.float32
    group = CORES * tasks * per
    buffers = [
        ((chips, 2, count, 128), f32),
        ((chunks, chips, count, chunk), bf16),
        ((chunks, tasks, experts, per, chunk), bf16),
        ((chunks, experts, CORES, tasks, per, chunk), bf16),
        ((experts, group, ff), f32),
        ((experts, group, ff), f32),
        ((experts, group, ff), bf16),
        ((chunks, experts, CORES, tasks, per, chunk), bf16),
        ((chunks, experts, tasks, per, chunk), bf16),
        ((chunks, experts, tasks, per, chunk), bf16),
        ((chunks, tasks, experts, per, chunk), bf16),
        ((chunks, chips, count, chunk), bf16),
        ((chunks, chips, count, chunk), bf16),
        ((UP_SLOTS, chunk, ff), bf16),
        ((DOWN_SLOTS, ff, chunk), bf16),
    ]
    size = sum(functools.reduce(lambda a, b: a * b, s) * jnp.dtype(d).itemsize for s, d in buffers)
    dma = pltpu.SemaphoreType.DMA
    sems = [dma((UP_SLOTS,)), dma((DOWN_SLOTS,)), dma((chips,)), dma((chips,))]
    sems += [dma((chunks, chips))] * 2 + [dma((chunks, tasks))] * 2 + [dma((chunks,))] * 5
    sems += [dma((chunks, tasks))] * 2 + [dma((chunks,))] + [dma((chunks, chips))] * 2
    return [pltpu.VMEM(s, d) for s, d in buffers] + sems, size


def fused(tokens, gain, task_ids, order, w_gate, w_up, w_down, scratch, chunk):
    tasks, chips = lax.axis_size("task"), lax.axis_size("shard") // CORES
    count, width = tokens.shape
    vmem = pl.BlockSpec(memory_space=pltpu.VMEM)
    hbm = pl.BlockSpec(memory_space=pl.ANY)
    return pl.pallas_call(
        functools.partial(layer_kernel, tasks, chips, chunk),
        out_shape=jax.ShapeDtypeStruct((count, width), jnp.bfloat16),
        in_specs=[vmem] * 4 + [hbm] * 3,
        out_specs=vmem,
        scratch_shapes=scratch,
        compiler_params=pltpu.CompilerParams(
            collective_id=0, has_side_effects=True, vmem_limit_bytes=VMEM_BYTES
        ),
        name="expert_layer",
    )(
        tokens, gain.reshape(1, width), task_ids.reshape(1, count), order.reshape(1, count),
        w_gate, w_up, w_down,
    )


def expert_block(gathered_rows, w_gate, w_up, w_down):
    gate_value = jnp.einsum(
        "red,edf->ref", gathered_rows, w_gate, preferred_element_type=jnp.float32
    )
    up_value = jnp.einsum("red,edf->ref", gathered_rows, w_up, preferred_element_type=jnp.float32)
    hidden = (jax.nn.silu(gate_value) * up_value).astype(jnp.bfloat16)
    return jnp.einsum("ref,efd->red", hidden, w_down, preferred_element_type=jnp.float32)


def collective(tokens, gain, task_ids, order, w_gate, w_up, w_down):
    task_count = lax.axis_size("task")
    local_experts = w_gate.shape[0]
    expert_count = task_count * local_experts
    feature_count = tokens.shape[1]
    values = tokens.astype(jnp.float32)
    mean_square = jnp.mean(values * values, axis=-1, keepdims=True)
    normed = (values * lax.rsqrt(mean_square + epsilon) * gain).astype(jnp.bfloat16)
    onehot = (task_ids[:, None] == jnp.arange(expert_count, dtype=jnp.int32)[None, :]).astype(
        jnp.int32
    )
    position = jnp.sum(jnp.cumsum(onehot, axis=0) * onehot, axis=1) - 1
    slot_index = (
        task_ids // local_experts * CAP + position
    ) * local_experts + task_ids % local_experts
    slot_count = task_count * CAP * local_experts
    slot_range = jnp.arange(slot_count, dtype=jnp.int32)
    placing = (slot_index[:, None] == slot_range[None, :]).astype(jnp.bfloat16)
    outgoing = jnp.einsum("rs,rd->sd", placing, normed, preferred_element_type=jnp.float32).astype(
        jnp.bfloat16
    )
    outgoing = outgoing.reshape(task_count, CAP, local_experts, feature_count)
    arrived = lax.all_to_all(outgoing, "task", split_axis=0, concat_axis=0, tiled=True)
    local_rows = arrived.reshape(task_count * CAP, local_experts, feature_count)
    partial_terms = expert_block(
        lax.all_gather(local_rows, "shard", axis=0, tiled=True), w_gate, w_up, w_down
    )
    summed = lax.psum_scatter(
        partial_terms.astype(jnp.bfloat16), "shard", scatter_dimension=0, tiled=True
    )
    results = summed.reshape(task_count, CAP, local_experts, feature_count)
    returned = lax.all_to_all(results, "task", split_axis=0, concat_axis=0, tiled=True)
    returned = returned.reshape(slot_count, feature_count)
    wanted = jnp.take(slot_index, order)
    selecting = (wanted[:, None] == slot_range[None, :]).astype(jnp.bfloat16)
    return jnp.dot(selecting, returned, preferred_element_type=jnp.float32).astype(jnp.bfloat16)


def shards(tokens, gain, task_ids, order, w_gate, w_up, w_down):
    tasks, shard_count = lax.axis_size("task"), lax.axis_size("shard")
    width = tokens.shape[1]
    chunk = CHUNK if width % CHUNK == 0 else width
    chips = shard_count // CORES
    scratch, size = scratch_of(tasks, chips, chunk, tokens, w_gate)
    arrays = (tokens, gain, task_ids, order, w_gate, w_up, w_down)
    if shard_count % CORES or chunk % 256 or size + 2 * 2**20 > VMEM_BYTES:
        return collective(*arrays)
    return fused(*arrays, scratch, chunk)


def solution(mesh):
    placed = (
        P(("task", "shard"), None),
        P(),
        P(("task", "shard")),
        P(("task", "shard")),
        P("task", None, "shard"),
        P("task", None, "shard"),
        P("task", "shard", None),
    )
    return jax.shard_map(
        shards, mesh=mesh, in_specs=placed, out_specs=P(("task", "shard"), None), check_vma=False
    )
```

```python
import functools

import jax
import jax.numpy as jnp
from jax import lax
from jax.experimental import pallas as pl
from jax.experimental.pallas import tpu as pltpu
from jax.sharding import PartitionSpec as P

MESH = pl.DeviceIdType.MESH
CAP = 8
CORES = 2
CHUNK = 1024
OUT_CHUNK = 512
UP_SLOTS = 6
DOWN_SLOTS = 6
AHEAD = 2
EARLY = 4
VMEM_BYTES = 63 * 2**20
epsilon = 1e-06


def tile_of(size):
    return 256 if size % 256 == 0 else size


def layer_kernel(
    tasks, chips, chunk, out_chunk,
    tokens, gain, task_row, order_row, w_gate, w_up, w_down, out,
    ids, rows, placed, x, gate_acc, up_acc, hidden, part, sib, pair, back, picked, terms, wbuf, dbuf,
    w_sem, d_sem, i_send, i_recv, z_send, z_recv, x_send, x_recv, x_local, b_send, b_recv,
    c_send, c_recv, y_send, y_recv, y_local, t_send, t_recv,
):
    experts, width, ff = w_gate.shape
    count = tokens.shape[0]
    chunks = width // chunk
    out_chunks = width // out_chunk
    per = chips * CAP
    slots = tasks * experts * per
    tile = tile_of(ff)
    me_t = lax.axis_index("task")
    me_s = lax.axis_index("shard")
    me_q = me_s // CORES
    me_c = me_s % CORES
    other_c = 1 - me_c
    sibling = (me_t, me_q * CORES + other_c)

    def chip_at(k):
        return lax.rem(me_q + k, chips)

    def task_at(k):
        return lax.rem(me_t + k, tasks)

    up_pieces = [(j, e, w) for j in range(chunks) for e in range(experts) for w in (w_gate, w_up)]
    down_pieces = [(j, e) for j in range(out_chunks) for e in range(experts)]

    def up_copy(i):
        j, e, w = up_pieces[i]
        slot = i % UP_SLOTS
        return pltpu.make_async_copy(
            w.at[e, pl.ds(j * chunk, chunk), :], wbuf.at[slot], w_sem.at[slot]
        )

    def down_copy(i):
        j, e = down_pieces[i]
        slot = i % DOWN_SLOTS
        return pltpu.make_async_copy(
            w_down.at[e, :, pl.ds(j * out_chunk, out_chunk)], dbuf.at[slot], d_sem.at[slot]
        )

    barrier = pltpu.get_barrier_semaphore()
    chip_peers = [(me_t, chip_at(k) * CORES + me_c) for k in range(1, chips)]
    task_peers = [(task_at(k), me_s) for k in range(1, tasks)]
    for peer in chip_peers + task_peers + [sibling]:
        pl.semaphore_signal(barrier, inc=1, device_id=peer, device_id_type=MESH)

    for i in range(min(EARLY, UP_SLOTS, len(up_pieces))):
        up_copy(i).start()

    first = lax.broadcasted_iota(jnp.int32, (count, count), 0)
    second = lax.broadcasted_iota(jnp.int32, (count, count), 1)
    task_line = task_row[...].astype(jnp.float32)
    order_line = order_row[...].astype(jnp.float32)

    def as_column(line):
        spread = jnp.broadcast_to(line, (count, count))
        return jnp.sum(jnp.where(first == second, spread, 0.0), axis=1, keepdims=True)

    task_col = as_column(task_line)
    order_col = as_column(order_line)
    col = jnp.broadcast_to(task_col, (count, count))
    row = jnp.broadcast_to(task_line, (count, count))
    same = col == row
    col_pos = jnp.sum(jnp.where(same & (second < first), 1.0, 0.0), axis=1, keepdims=True)
    row_pos = jnp.sum(jnp.where(same & (first < second), 1.0, 0.0), axis=0, keepdims=True)
    col_id = task_col * CAP + col_pos
    row_id = task_line * CAP + row_pos
    taken = jnp.broadcast_to(order_col, (count, count)) == second.astype(jnp.float32)
    want_id = jnp.sum(
        jnp.where(taken, jnp.broadcast_to(row_id, (count, count)), 0.0), axis=1, keepdims=True
    )
    ids[me_q, 0] = jnp.broadcast_to(col_id, (count, 128))
    ids[me_q, 1] = jnp.broadcast_to(want_id, (count, 128))

    values = tokens[...].astype(jnp.float32)
    mean_square = jnp.mean(values * values, axis=-1, keepdims=True)
    scale = lax.rsqrt(mean_square + epsilon)
    for j in range(chunks):
        part_cols = pl.ds(j * chunk, chunk)
        rows[j, me_q] = (
            tokens[:, part_cols].astype(jnp.float32) * scale * gain[:, part_cols]
        ).astype(jnp.bfloat16)

    pl.semaphore_wait(barrier, len(chip_peers) + len(task_peers) + 1)

    sends = []

    def remote(src, dst, send, recv, peer):
        copy = pltpu.make_async_remote_copy(
            src_ref=src, dst_ref=dst, send_sem=send, recv_sem=recv,
            device_id=peer, device_id_type=MESH,
        )
        copy.start()
        sends.append(copy)
        return copy

    id_copies = [
        remote(ids.at[me_q], ids.at[me_q], i_send.at[k], i_recv.at[k], peer)
        for k, peer in enumerate(chip_peers)
    ]
    row_copies = {}

    def send_rows(j):
        row_copies[j] = [
            remote(rows.at[j, me_q], rows.at[j, me_q], z_send.at[j, k], z_recv.at[j, k], peer)
            for k, peer in enumerate(chip_peers)
        ]

    for j in range(min(AHEAD, chunks)):
        send_rows(j)

    for i in range(EARLY, min(UP_SLOTS, len(up_pieces))):
        up_copy(i).start()
    for i in range(min(DOWN_SLOTS, len(down_pieces))):
        down_copy(i).start()

    for copy in id_copies:
        copy.wait_recv()
    shape = (chips * count, slots)
    lane = lax.broadcasted_iota(jnp.int32, shape, 1)
    line = lax.broadcasted_iota(jnp.int32, shape, 0)
    lane_id = ((lane // per) * CAP + lane % CAP).astype(jnp.float32)
    mine = (lane // CAP) % chips == line // count

    def one_hot(which):
        held = ids[:, which].reshape(chips * count, 128)[:, :1]
        hit = (jnp.broadcast_to(held, shape) == lane_id) & mine
        return jnp.where(hit, 1.0, 0.0)

    placing = one_hot(0).T.astype(jnp.bfloat16)
    picking = one_hot(1).astype(jnp.bfloat16)

    cross, swaps, pair_swaps, returns, finals = {}, {}, {}, {}, {}

    def place(j):
        for copy in row_copies[j]:
            copy.wait_recv()
        if j + AHEAD < chunks:
            send_rows(j + AHEAD)
        for n in range(0, chunk, 256):
            got = jnp.dot(
                placing,
                rows[j, :, :, n : n + 256].reshape(chips * count, 256),
                preferred_element_type=jnp.float32,
            ).astype(jnp.bfloat16)
            placed[j, :, :, :, n : n + 256] = got.reshape(tasks, experts, per, 256)
        cross[j] = [
            remote(
                placed.at[j, peer[0]], x.at[j, :, me_c, me_t],
                x_send.at[j, k], x_recv.at[j, k], peer,
            )
            for k, peer in enumerate(task_peers)
        ]
        local = pltpu.make_async_copy(
            placed.at[j, me_t], x.at[j, :, me_c, me_t], x_local.at[j]
        )
        local.start()
        cross[j].append(local)

    def swap(j):
        for copy in cross[j][:-1]:
            copy.wait_recv()
        cross[j][-1].wait()
        swaps[j] = remote(
            x.at[j, :, me_c], x.at[j, :, me_c], b_send.at[j], b_recv.at[j], sibling
        )

    def enter(j):
        swaps[j].wait_recv()
        for e in range(experts):
            i = (j * experts + e) * 2
            up_copy(i).wait()
            up_copy(i + 1).wait()

            def step(n, carry):
                columns = pl.ds(pl.multiple_of(n * tile, tile), tile)
                block = x[j, e].reshape(CORES * tasks * per, chunk)
                g = jnp.dot(
                    block, wbuf[i % UP_SLOTS, :, columns], preferred_element_type=jnp.float32
                )
                u = jnp.dot(
                    block, wbuf[(i + 1) % UP_SLOTS, :, columns], preferred_element_type=jnp.float32
                )
                if j > 0:
                    g += gate_acc[e, :, columns]
                    u += up_acc[e, :, columns]
                if j < chunks - 1:
                    gate_acc[e, :, columns] = g
                    up_acc[e, :, columns] = u
                else:
                    hidden[e, :, columns] = (g / (1.0 + jnp.exp(-g)) * u).astype(jnp.bfloat16)
                return carry

            lax.fori_loop(0, ff // tile, step, 0)
            for later in (i + UP_SLOTS, i + 1 + UP_SLOTS):
                if later < len(up_pieces):
                    up_copy(later).start()

    def leave(j):
        for e in range(experts):
            i = j * experts + e
            down_copy(i).wait()

            got = jnp.dot(
                hidden[e], dbuf[i % DOWN_SLOTS], preferred_element_type=jnp.float32
            ).astype(jnp.bfloat16)
            part[j, e] = got.reshape(CORES, tasks, per, out_chunk)
            if i + DOWN_SLOTS < len(down_pieces):
                down_copy(i + DOWN_SLOTS).start()
        pair_swaps[j] = remote(
            part.at[j, :, other_c], sib.at[j], c_send.at[j], c_recv.at[j], sibling
        )

    def add_pair(j):
        pair_swaps[j].wait_recv()
        for e in range(experts):
            for t in range(tasks):
                pair[j, e, t] = (
                    part[j, e, me_c, t].astype(jnp.float32) + sib[j, e, t].astype(jnp.float32)
                ).astype(jnp.bfloat16)
        returns[j] = [
            remote(
                pair.at[j, :, peer[0]], back.at[j, me_t], y_send.at[j, k], y_recv.at[j, k], peer
            )
            for k, peer in enumerate(task_peers)
        ]
        local = pltpu.make_async_copy(pair.at[j, :, me_t], back.at[j, me_t], y_local.at[j])
        local.start()
        returns[j].append(local)

    def pick(j):
        for copy in returns[j][:-1]:
            copy.wait_recv()
        returns[j][-1].wait()
        for n in range(0, out_chunk, 256):
            got = jnp.dot(
                picking,
                back[j, :, :, :, n : n + 256].reshape(slots, 256),
                preferred_element_type=jnp.float32,
            ).astype(jnp.bfloat16)
            picked[j, :, :, n : n + 256] = got.reshape(chips, count, 256)
        finals[j] = [
            remote(
                picked.at[j, chip_at(k + 1)], terms.at[j, me_q],
                t_send.at[j, k], t_recv.at[j, k], peer,
            )
            for k, peer in enumerate(chip_peers)
        ]
        terms[j, me_q] = picked[j, me_q]

    def finish(j):
        for copy in finals[j]:
            copy.wait_recv()
        total = terms[j, 0].astype(jnp.float32)
        for k in range(1, chips):
            total += terms[j, k].astype(jnp.float32)
        out[:, pl.ds(j * out_chunk, out_chunk)] = total.astype(jnp.bfloat16)

    for step in range(chunks + 2):
        if step < chunks:
            place(step)
        if 0 <= step - 1 < chunks:
            swap(step - 1)
        if 0 <= step - 2 < chunks:
            enter(step - 2)
    for step in range(out_chunks + 3):
        if step < out_chunks:
            leave(step)
        if 0 <= step - 1 < out_chunks:
            add_pair(step - 1)
        if 0 <= step - 2 < out_chunks:
            pick(step - 2)
        if 0 <= step - 3 < out_chunks:
            finish(step - 3)
    for copy in sends:
        copy.wait_send()


def scratch_of(tasks, chips, chunk, out_chunk, tokens, w_gate):
    experts, width, ff = w_gate.shape
    count = tokens.shape[0]
    chunks, out_chunks, per = width // chunk, width // out_chunk, chips * CAP
    bf16, f32 = jnp.bfloat16, jnp.float32
    group = CORES * tasks * per
    buffers = [
        ((chips, 2, count, 128), f32),
        ((chunks, chips, count, chunk), bf16),
        ((chunks, tasks, experts, per, chunk), bf16),
        ((chunks, experts, CORES, tasks, per, chunk), bf16),
        ((experts, group, ff), f32),
        ((experts, group, ff), f32),
        ((experts, group, ff), bf16),
        ((out_chunks, experts, CORES, tasks, per, out_chunk), bf16),
        ((out_chunks, experts, tasks, per, out_chunk), bf16),
        ((out_chunks, experts, tasks, per, out_chunk), bf16),
        ((out_chunks, tasks, experts, per, out_chunk), bf16),
        ((out_chunks, chips, count, out_chunk), bf16),
        ((out_chunks, chips, count, out_chunk), bf16),
        ((UP_SLOTS, chunk, ff), bf16),
        ((DOWN_SLOTS, ff, out_chunk), bf16),
    ]
    size = sum(functools.reduce(lambda a, b: a * b, s) * jnp.dtype(d).itemsize for s, d in buffers)
    dma = pltpu.SemaphoreType.DMA
    sems = [dma((UP_SLOTS,)), dma((DOWN_SLOTS,)), dma((chips,)), dma((chips,))]
    sems += [dma((chunks, chips))] * 2 + [dma((chunks, tasks))] * 2 + [dma((chunks,))] * 3
    sems += [dma((out_chunks,))] * 2 + [dma((out_chunks, tasks))] * 2
    sems += [dma((out_chunks,))] + [dma((out_chunks, chips))] * 2
    return [pltpu.VMEM(s, d) for s, d in buffers] + sems, size


def fused(tokens, gain, task_ids, order, w_gate, w_up, w_down, scratch, chunk, out_chunk):
    tasks, chips = lax.axis_size("task"), lax.axis_size("shard") // CORES
    count, width = tokens.shape
    vmem = pl.BlockSpec(memory_space=pltpu.VMEM)
    hbm = pl.BlockSpec(memory_space=pl.ANY)
    return pl.pallas_call(
        functools.partial(layer_kernel, tasks, chips, chunk, out_chunk),
        out_shape=jax.ShapeDtypeStruct((count, width), jnp.bfloat16),
        in_specs=[vmem] * 4 + [hbm] * 3,
        out_specs=vmem,
        scratch_shapes=scratch,
        compiler_params=pltpu.CompilerParams(
            collective_id=0, has_side_effects=True, vmem_limit_bytes=VMEM_BYTES
        ),
        name="expert_layer",
    )(
        tokens, gain.reshape(1, width), task_ids.reshape(1, count), order.reshape(1, count),
        w_gate, w_up, w_down,
    )


def expert_block(gathered_rows, w_gate, w_up, w_down):
    gate_value = jnp.einsum(
        "red,edf->ref", gathered_rows, w_gate, preferred_element_type=jnp.float32
    )
    up_value = jnp.einsum("red,edf->ref", gathered_rows, w_up, preferred_element_type=jnp.float32)
    hidden = (jax.nn.silu(gate_value) * up_value).astype(jnp.bfloat16)
    return jnp.einsum("ref,efd->red", hidden, w_down, preferred_element_type=jnp.float32)


def collective(tokens, gain, task_ids, order, w_gate, w_up, w_down):
    task_count = lax.axis_size("task")
    local_experts = w_gate.shape[0]
    expert_count = task_count * local_experts
    feature_count = tokens.shape[1]
    values = tokens.astype(jnp.float32)
    mean_square = jnp.mean(values * values, axis=-1, keepdims=True)
    normed = (values * lax.rsqrt(mean_square + epsilon) * gain).astype(jnp.bfloat16)
    onehot = (task_ids[:, None] == jnp.arange(expert_count, dtype=jnp.int32)[None, :]).astype(
        jnp.int32
    )
    position = jnp.sum(jnp.cumsum(onehot, axis=0) * onehot, axis=1) - 1
    slot_index = (
        task_ids // local_experts * CAP + position
    ) * local_experts + task_ids % local_experts
    slot_count = task_count * CAP * local_experts
    slot_range = jnp.arange(slot_count, dtype=jnp.int32)
    placing = (slot_index[:, None] == slot_range[None, :]).astype(jnp.bfloat16)
    outgoing = jnp.einsum("rs,rd->sd", placing, normed, preferred_element_type=jnp.float32).astype(
        jnp.bfloat16
    )
    outgoing = outgoing.reshape(task_count, CAP, local_experts, feature_count)
    arrived = lax.all_to_all(outgoing, "task", split_axis=0, concat_axis=0, tiled=True)
    local_rows = arrived.reshape(task_count * CAP, local_experts, feature_count)
    partial_terms = expert_block(
        lax.all_gather(local_rows, "shard", axis=0, tiled=True), w_gate, w_up, w_down
    )
    summed = lax.psum_scatter(
        partial_terms.astype(jnp.bfloat16), "shard", scatter_dimension=0, tiled=True
    )
    results = summed.reshape(task_count, CAP, local_experts, feature_count)
    returned = lax.all_to_all(results, "task", split_axis=0, concat_axis=0, tiled=True)
    returned = returned.reshape(slot_count, feature_count)
    wanted = jnp.take(slot_index, order)
    selecting = (wanted[:, None] == slot_range[None, :]).astype(jnp.bfloat16)
    return jnp.dot(selecting, returned, preferred_element_type=jnp.float32).astype(jnp.bfloat16)


def shards(tokens, gain, task_ids, order, w_gate, w_up, w_down):
    tasks, shard_count = lax.axis_size("task"), lax.axis_size("shard")
    width = tokens.shape[1]
    chunk = CHUNK if width % CHUNK == 0 else width
    out_chunk = OUT_CHUNK if width % OUT_CHUNK == 0 else width
    chips = shard_count // CORES
    scratch, size = scratch_of(tasks, chips, chunk, out_chunk, tokens, w_gate)
    arrays = (tokens, gain, task_ids, order, w_gate, w_up, w_down)
    if shard_count % CORES or chunk % 256 or out_chunk % 256 or size + 2 * 2**20 > VMEM_BYTES:
        return collective(*arrays)
    return fused(*arrays, scratch, chunk, out_chunk)


def solution(mesh):
    placed = (
        P(("task", "shard"), None),
        P(),
        P(("task", "shard")),
        P(("task", "shard")),
        P("task", None, "shard"),
        P("task", None, "shard"),
        P("task", "shard", None),
    )
    return jax.shard_map(
        shards, mesh=mesh, in_specs=placed, out_specs=P(("task", "shard"), None), check_vma=False
    )
```
